1024 devices in a mesh: ctx: 256 (over x, y_hi, z), head: 4 (over y_lo, core).
Axes of the slice: x: 4, y: 8 (y_hi: 4, y_lo: 2; y = y_hi * 2 + y_lo), z: 16, core: 2. Of those that a mesh axis runs over, the one named last changes fastest.
Arguments:
- queries: bfloat16 [32768, 8, 4, 128], P('ctx', 'head'), may hold values from -8 to 8
- keys: bfloat16 [32768, 4, 128], P('ctx'), may hold values from -8 to 8
- values: bfloat16 [32768, 4, 128], P('ctx'), may hold values from -6 to 6
- out_grad: bfloat16 [32768, 8, 4, 128], P('ctx', 'head'), may hold values from -6 to 6
- lengths: int32 [128], replicated, may hold values from 1 to 384, as said below
Outputs:
- query_grad: bfloat16 [32768, 8, 4, 128], P('ctx', 'head')
- key_grad: bfloat16 [32768, 4, 128], P('ctx', 'head')
- value_grad: bfloat16 [32768, 4, 128], P('ctx', 'head')
The draws below stay inside these ranges and needn't reach their ends.
Inputs may be any that keep to these rules, and one draw needn't show every extreme that they name: The 128 lengths sum to 32768; the first document is the longest, exactly 384 tokens.
All inputs are finite; a program needn't handle non-finite values.
Results may differ from the reference program's by a relative error of at most 0.008.
Values may be sent and summed in bfloat16 or wider, within the bound.
A program may use at most 32 MiB of HBM per device.

```python
import jax
import jax.numpy as jnp
from jax import lax

HD = 128
QPG = 8
KV = 4
TOK_DEV = 128
SPAN = 4
TOKENS = 32768
DOCS = 128
MAXDOC = 384


def draw_keys(key, part):
    key = jax.random.fold_in(key, 1)
    result = jnp.clip(jax.random.normal(key, (TOKENS, KV, HD), jnp.float32), -8.0, 8.0)
    return result.astype(jnp.bfloat16)


def draw_queries(key, part):
    key = jax.random.fold_in(key, 2)
    result = jnp.clip(jax.random.normal(key, (TOKENS, QPG, KV, HD), jnp.float32), -8.0, 8.0)
    return result.astype(jnp.bfloat16)


def draw_lengths(key, part):
    key = jax.random.fold_in(key, 3)
    pair_count = (DOCS - 2) // 2
    shorter = jax.random.randint(jax.random.fold_in(key, 1), (pair_count,), TOK_DEV, 3 * TOK_DEV + 1).astype(jnp.int32)
    longer = (4 * TOK_DEV - shorter).astype(jnp.int32)
    rest = jnp.concatenate([shorter, longer, jnp.full((1,), TOK_DEV, jnp.int32)], 0)
    order = jax.random.permutation(jax.random.fold_in(key, 2), DOCS - 1)
    rest = rest[order]
    return jnp.concatenate([jnp.full((1,), MAXDOC, jnp.int32), rest], 0).astype(jnp.int32)


def levels(key, extent, split, least, largest):
    factor_of, own = 1.0, jax.random.fold_in(key, 6)
    for dim, shards_of in split:
        heights = jnp.exp(jax.random.uniform(jax.random.fold_in(own, dim), (shards_of,), jnp.float32, least / len(split), largest / len(split)))
        factor_of = factor_of * jnp.repeat(heights, extent[dim] // shards_of).reshape([-1 if axis == dim else 1 for axis in range(len(extent))])
    return factor_of


def gaussian(key, shape, deviation, bound, cuts=(), kind=jnp.bfloat16):
    factor_of = levels(key, shape, cuts, -0.22, 0.18) if cuts else 1.0
    entries = jax.random.normal(key, shape, jnp.float32) * deviation * factor_of
    return jnp.minimum(jnp.maximum(entries, -bound), bound).astype(kind)


def setup_inputs(seed: int = 0) -> dict:
    streams_of = jax.random.split(jax.random.key(seed), 6)
    return {
        "queries": draw_queries(jax.random.fold_in(streams_of[5], 71), 0),
        "keys": draw_keys(jax.random.fold_in(streams_of[5], 71), 0),
        "values": gaussian(streams_of[2], (TOKENS, KV, HD), 1.0, 6.0, ((0, 256),)),
        "out_grad": gaussian(streams_of[3], (TOKENS, QPG, KV, HD), 1.0, 6.0, ((0, 256), (1, 4))),
        "lengths": draw_lengths(jax.random.fold_in(streams_of[5], 71), 0),
    }


lowest = -1e30


def doc_of(lengths, position):
    ends = jnp.cumsum(lengths).astype(jnp.int32)
    return jnp.sum((ends[None, :] <= position[:, None]).astype(jnp.int32), axis=1).astype(jnp.int32)


def rounded(array):
    return lax.optimization_barrier(array.astype(jnp.bfloat16)).astype(jnp.float32)


def reference(queries, keys, values, out_grad, lengths):
    factor = HD ** -0.5
    width = TOK_DEV
    blocks = TOKENS // width
    window = SPAN * width
    margin = (SPAN - 1) * width
    position = jnp.arange(TOKENS, dtype=jnp.int32)
    document = doc_of(lengths, position)
    keys_pad = jnp.concatenate([jnp.zeros((margin, KV, HD), keys.dtype), keys], 0)
    values_pad = jnp.concatenate([jnp.zeros((margin, KV, HD), values.dtype), values], 0)
    key_pos = jnp.concatenate([jnp.full((margin,), -1, jnp.int32), position], 0)
    key_doc = jnp.concatenate([jnp.full((margin,), -1, jnp.int32), document], 0)

    def first(index):
        start = (index * width).astype(jnp.int32)
        q_block = lax.dynamic_slice_in_dim(queries, start, width, 0).astype(jnp.float32)
        g_block = lax.dynamic_slice_in_dim(out_grad, start, width, 0).astype(jnp.float32)
        k_window = lax.dynamic_slice_in_dim(keys_pad, start, window, 0).astype(jnp.float32)
        v_window = lax.dynamic_slice_in_dim(values_pad, start, window, 0).astype(jnp.float32)
        q_pos = lax.dynamic_slice_in_dim(position, start, width, 0)
        q_doc = lax.dynamic_slice_in_dim(document, start, width, 0)
        k_pos = lax.dynamic_slice_in_dim(key_pos, start, window, 0)
        k_doc = lax.dynamic_slice_in_dim(key_doc, start, window, 0)
        allowed = (k_pos[None, :] <= q_pos[:, None]) & (k_doc[None, :] == q_doc[:, None])
        wide_mask = allowed[:, None, None, :]
        score = jnp.einsum("pjgd,tgd->pjgt", q_block, k_window) * factor
        peak = jnp.max(jnp.where(wide_mask, score, lowest), axis=-1)
        expo = jnp.where(wide_mask, jnp.exp(score - peak[..., None]), 0.0)
        total = jnp.sum(expo, axis=-1)
        dprob = jnp.einsum("pjgd,tgd->pjgt", g_block, v_window)
        delta = jnp.sum(expo * dprob, axis=-1) / total
        prob = jnp.where(wide_mask, jnp.exp(score - peak[..., None]) / total[..., None], 0.0)
        dscore = rounded(prob * (dprob - delta[..., None]))
        query_grad = jnp.einsum("pjgt,tgd->pjgd", dscore, k_window) * factor
        return query_grad.astype(jnp.bfloat16), peak, total, delta

    query_grad, peak, total, delta = lax.map(first, jnp.arange(blocks, dtype=jnp.int32))
    query_grad = query_grad.reshape(TOKENS, QPG, KV, HD)
    peak = peak.reshape(TOKENS, QPG, KV)
    total = total.reshape(TOKENS, QPG, KV)
    delta = delta.reshape(TOKENS, QPG, KV)

    queries_pad = jnp.concatenate([queries, jnp.zeros((margin, QPG, KV, HD), queries.dtype)], 0)
    grad_pad = jnp.concatenate([out_grad, jnp.zeros((margin, QPG, KV, HD), out_grad.dtype)], 0)
    peak_pad = jnp.concatenate([peak, jnp.zeros((margin, QPG, KV), jnp.float32)], 0)
    total_pad = jnp.concatenate([total, jnp.ones((margin, QPG, KV), jnp.float32)], 0)
    delta_pad = jnp.concatenate([delta, jnp.zeros((margin, QPG, KV), jnp.float32)], 0)
    query_pos = jnp.concatenate([position, TOKENS + jnp.arange(margin, dtype=jnp.int32)], 0)
    query_doc = jnp.concatenate([document, jnp.full((margin,), -2, jnp.int32)], 0)

    def second(index):
        start = (index * width).astype(jnp.int32)
        k_block = lax.dynamic_slice_in_dim(keys, start, width, 0).astype(jnp.float32)
        v_block = lax.dynamic_slice_in_dim(values, start, width, 0).astype(jnp.float32)
        k_pos = lax.dynamic_slice_in_dim(position, start, width, 0)
        k_doc = lax.dynamic_slice_in_dim(document, start, width, 0)
        q_window = lax.dynamic_slice_in_dim(queries_pad, start, window, 0).astype(jnp.float32)
        g_window = lax.dynamic_slice_in_dim(grad_pad, start, window, 0).astype(jnp.float32)
        p_window = lax.dynamic_slice_in_dim(peak_pad, start, window, 0)
        t_window = lax.dynamic_slice_in_dim(total_pad, start, window, 0)
        d_window = lax.dynamic_slice_in_dim(delta_pad, start, window, 0)
        q_pos = lax.dynamic_slice_in_dim(query_pos, start, window, 0)
        q_doc = lax.dynamic_slice_in_dim(query_doc, start, window, 0)
        allowed = (k_pos[None, :] <= q_pos[:, None]) & (k_doc[None, :] == q_doc[:, None])
        wide_mask = allowed[:, None, None, :]
        score = jnp.einsum("pjgd,tgd->pjgt", q_window, k_block) * factor
        prob = jnp.where(wide_mask, jnp.exp(score - p_window[..., None]) / t_window[..., None], 0.0)
        dprob = jnp.einsum("pjgd,tgd->pjgt", g_window, v_block)
        dscore = rounded(prob * (dprob - d_window[..., None]))
        prob_low = rounded(prob)
        key_grad = jnp.einsum("pjgt,pjgd->tgd", dscore, q_window) * factor
        value_grad = jnp.einsum("pjgt,pjgd->tgd", prob_low, g_window)
        return key_grad.astype(jnp.bfloat16), value_grad.astype(jnp.bfloat16)

    key_grad, value_grad = lax.map(second, jnp.arange(blocks, dtype=jnp.int32))
    return query_grad, key_grad.reshape(TOKENS, KV, HD), value_grad.reshape(TOKENS, KV, HD)
```

```python
import jax
import jax.numpy as jnp
from jax import lax
from jax.experimental import pallas as pl
from jax.experimental.pallas import tpu as pltpu
from jax.sharding import PartitionSpec as P

SPAN = 4
HEADS = 4
LOWEST = -1e30
LOG2E = 1.4426950408889634
MESH = pl.DeviceIdType.MESH
NT = (((1,), (1,)), ((), ()))


def kernel(
    len_ref, qo_ref, kv_ref,
    dq_ref, dkv_ref,
    qo_all, kv_all, kt_all, e_all, dp_all, ds_all, m_all, t_all, w_all, g_out, g_in, dq_out,
    qo_send, qo_recv, kv_send, kv_recv, g_send, g_recv, dq_send, dq_recv,
):
    ctx = lax.axis_index("ctx")
    head = lax.axis_index("head")
    count = lax.axis_size("ctx")
    width = kv_ref.shape[1]
    depth = kv_ref.shape[2]
    rows = qo_ref.shape[2]
    factor = depth ** -0.5

    def ctx_at(shift):
        return lax.rem(ctx + (shift + count), count)

    def head_at(shift):
        return lax.rem(head + (shift + HEADS), HEADS)

    barrier = pltpu.get_barrier_semaphore()
    for s in range(1, SPAN):
        for sign in (1, -1):
            pl.semaphore_signal(
                barrier, inc=1, device_id={"ctx": ctx_at(sign * s), "head": head}, device_id_type=MESH
            )
    for k in range(1, HEADS):
        pl.semaphore_signal(
            barrier, inc=1, device_id={"ctx": ctx, "head": head_at(k)}, device_id_type=MESH
        )
    pl.semaphore_wait(barrier, 2 * (SPAN - 1) + HEADS - 1)

    kv_copies = []
    for s in range(1, SPAN):
        copy = pltpu.make_async_remote_copy(
            src_ref=kv_ref, dst_ref=kv_all.at[s - 1],
            send_sem=kv_send.at[s - 1], recv_sem=kv_recv.at[s - 1],
            device_id={"ctx": ctx_at(s), "head": head}, device_id_type=MESH,
        )
        copy.start()
        kv_copies.append(copy)
    qo_copies = []
    for k in range(1, HEADS):
        target = head_at(k)
        copy = pltpu.make_async_remote_copy(
            src_ref=qo_ref.at[target], dst_ref=qo_all.at[k - 1],
            send_sem=qo_send.at[k - 1], recv_sem=qo_recv.at[k - 1],
            device_id={"ctx": ctx, "head": target}, device_id_type=MESH,
        )
        copy.start()
        qo_copies.append(copy)

    lengths = len_ref[...]
    down = lax.broadcasted_iota(jnp.int32, (width, width), 0)
    across = lax.broadcasted_iota(jnp.int32, (width, width), 1)
    spread = jnp.broadcast_to(lengths, (width, width)).astype(jnp.float32)
    ends = jnp.sum(jnp.where(across <= down, spread, 0.0), axis=1, keepdims=True)
    own = jnp.sum(jnp.where(across == down, spread, 0.0), axis=1, keepdims=True)
    query_pos = ctx * width + across
    start = jnp.sum(
        jnp.where(ends <= query_pos.astype(jnp.float32), own, 0.0), axis=0, keepdims=True
    ).astype(jnp.int32)

    def qo(k):
        return qo_ref.at[head] if k == 0 else qo_all.at[k - 1]

    def kv(s):
        return kv_ref if s == 0 else kv_all.at[s - 1]

    scale = factor * LOG2E
    for s in range(SPAN):
        if s:
            kv_copies[s - 1].wait_recv()
        keys = kv(s)[0]
        values = kv(s)[1]
        kt_all[:, s * width:(s + 1) * width] = keys.T
        key_pos = (ctx - s) * width + down
        allowed = (key_pos >= start) & (key_pos <= query_pos)
        bias = jnp.where(allowed, 0.0, LOWEST)
        bias = jnp.concatenate([bias] * (rows // width), axis=1)
        for k in range(HEADS):
            if s == 0 and k:
                qo_copies[k - 1].wait_recv()
            cols = slice(k * rows, (k + 1) * rows)
            score = lax.dot_general(keys, qo(k)[0], NT, preferred_element_type=jnp.float32) + bias
            dprob = lax.dot_general(values, qo(k)[1], NT, preferred_element_type=jnp.float32)
            peak = jnp.max(score, axis=0, keepdims=True)
            expo = jnp.exp2((score - peak) * scale)
            m_all[s, :, cols] = peak
            t_all[s, :, cols] = jnp.sum(expo, axis=0, keepdims=True)
            w_all[s, :, cols] = jnp.sum(expo * dprob, axis=0, keepdims=True)
            e_all[s, :, cols] = expo
            dp_all[s, :, cols] = dprob

    peaks = [m_all[s] for s in range(SPAN)]
    peak = jnp.maximum(jnp.maximum(peaks[0], peaks[1]), jnp.maximum(peaks[2], peaks[3]))
    shares = [jnp.exp2((p - peak) * scale) for p in peaks]
    total = sum(t_all[s] * shares[s] for s in range(SPAN))
    inverse = 1.0 / total
    delta = sum(w_all[s] * shares[s] for s in range(SPAN)) * inverse
    shares = [share * inverse for share in shares]

    g_copies = []
    mine = None
    for s in (3, 2, 1, 0):
        keys_part = jnp.zeros((width, depth), jnp.float32)
        values_part = jnp.zeros((width, depth), jnp.float32)
        for k in range(HEADS):
            cols = slice(k * rows, (k + 1) * rows)
            prob = e_all[s, :, cols] * shares[s][:, cols]
            dscore = (prob * (dp_all[s, :, cols] - delta[:, cols])).astype(jnp.bfloat16)
            ds_all[s * width:(s + 1) * width, cols] = dscore
            keys_part += jnp.dot(dscore, qo(k)[0], preferred_element_type=jnp.float32)
            values_part += jnp.dot(
                prob.astype(jnp.bfloat16), qo(k)[1], preferred_element_type=jnp.float32
            )
        keys_part = keys_part * factor
        if s:
            g_out[s - 1, 0] = keys_part.astype(jnp.bfloat16)
            g_out[s - 1, 1] = values_part.astype(jnp.bfloat16)
            copy = pltpu.make_async_remote_copy(
                src_ref=g_out.at[s - 1], dst_ref=g_in.at[s - 1],
                send_sem=g_send.at[s - 1], recv_sem=g_recv.at[s - 1],
                device_id={"ctx": ctx_at(-s), "head": head}, device_id_type=MESH,
            )
            copy.start()
            g_copies.append(copy)
        else:
            mine = (keys_part, values_part)

    dq_copies = []
    for k in (1, 2, 3, 0):
        cols = slice(k * rows, (k + 1) * rows)
        dq = jnp.dot(kt_all[...], ds_all[:, cols], preferred_element_type=jnp.float32)
        dq = (dq.T * factor).astype(jnp.bfloat16)
        if k:
            dq_out[k - 1] = dq
            copy = pltpu.make_async_remote_copy(
                src_ref=dq_out.at[k - 1], dst_ref=dq_ref.at[head],
                send_sem=dq_send.at[k - 1], recv_sem=dq_recv.at[k - 1],
                device_id={"ctx": ctx, "head": head_at(-k)}, device_id_type=MESH,
            )
            copy.start()
            dq_copies.append(copy)
        else:
            dq_ref[head] = dq

    for copy in g_copies:
        copy.wait_recv()
    for i in range(2):
        acc = mine[i]
        for s in range(1, SPAN):
            acc = acc + g_in[s - 1, i].astype(jnp.float32)
        dkv_ref[i] = acc.astype(jnp.bfloat16)
    for k, copy in zip((1, 2, 3), dq_copies):
        pltpu.make_async_remote_copy(
            src_ref=dq_out.at[k - 1], dst_ref=dq_ref.at[head_at(k)],
            send_sem=dq_send.at[k - 1], recv_sem=dq_recv.at[k - 1],
            device_id={"ctx": ctx, "head": head_at(-k)}, device_id_type=MESH,
        ).wait_recv()
    for copy in kv_copies + qo_copies + g_copies + dq_copies:
        copy.wait_send()


def on_device(queries, keys, values, out_grad, lengths):
    width, group, heads, depth = queries.shape
    head = lax.axis_index("head")
    rows = group * width
    qo = jnp.stack([queries, out_grad]).transpose(3, 0, 2, 1, 4).reshape(heads, 2, rows, depth)
    kv = jnp.stack([
        lax.dynamic_index_in_dim(keys, head, 1, keepdims=False),
        lax.dynamic_index_in_dim(values, head, 1, keepdims=False),
    ])
    vmem = pl.BlockSpec(memory_space=pltpu.VMEM)
    bf16, f32 = jnp.bfloat16, jnp.float32
    total_q = HEADS * rows
    dma = pltpu.SemaphoreType.DMA((3,))
    dq, dkv = pl.pallas_call(
        kernel,
        out_shape=(
            jax.ShapeDtypeStruct((heads, rows, depth), bf16),
            jax.ShapeDtypeStruct((2, width, depth), bf16),
        ),
        in_specs=[vmem] * 3,
        out_specs=(vmem, vmem),
        scratch_shapes=[
            pltpu.VMEM((HEADS - 1, 2, rows, depth), bf16),
            pltpu.VMEM((SPAN - 1, 2, width, depth), bf16),
            pltpu.VMEM((depth, SPAN * width), bf16),
            pltpu.VMEM((SPAN, width, total_q), f32),
            pltpu.VMEM((SPAN, width, total_q), f32),
            pltpu.VMEM((SPAN * width, total_q), bf16),
            pltpu.VMEM((SPAN, 1, total_q), f32),
            pltpu.VMEM((SPAN, 1, total_q), f32),
            pltpu.VMEM((SPAN, 1, total_q), f32),
            pltpu.VMEM((SPAN - 1, 2, width, depth), bf16),
            pltpu.VMEM((SPAN - 1, 2, width, depth), bf16),
            pltpu.VMEM((HEADS - 1, rows, depth), bf16),
        ] + [dma] * 8,
        compiler_params=pltpu.CompilerParams(
            collective_id=0, has_side_effects=True, vmem_limit_bytes=32 * 2 ** 20
        ),
    )(lengths.reshape(1, -1), qo, kv)
    query_grad = dq.reshape(heads, group, width, depth).transpose(2, 1, 0, 3)
    return query_grad, dkv[0][:, None, :], dkv[1][:, None, :]


def solution(mesh):
    in_specs = (
        P("ctx", "head", None, None),
        P("ctx", None, None),
        P("ctx", None, None),
        P("ctx", "head", None, None),
        P(),
    )
    out_specs = (P("ctx", "head", None, None), P("ctx", "head", None), P("ctx", "head", None))
    return jax.shard_map(
        on_device, mesh=mesh, in_specs=in_specs, out_specs=out_specs, check_vma=False
    )
```

```python
import jax
import jax.numpy as jnp
from jax import lax
from jax.experimental import pallas as pl
from jax.experimental.pallas import tpu as pltpu
from jax.sharding import PartitionSpec as P

SPAN = 4
HEADS = 4
LOWEST = -1e30
LOG2E = 1.4426950408889634
MESH = pl.DeviceIdType.MESH
NT = (((1,), (1,)), ((), ()))
BF16, F32, I32 = jnp.bfloat16, jnp.float32, jnp.int32


def one_hot(shape, column_of_row):
    row = lax.broadcasted_iota(I32, shape, 0)
    column = lax.broadcasted_iota(I32, shape, 1)
    return jnp.where(column == column_of_row(row), 1.0, 0.0).astype(BF16)


def kernel(
    len_hbm, q_hbm, k_hbm, v_hbm, o_hbm,
    dq_ref, dk_ref, dv_ref,
    len_in, q_in, k_in, v_in, o_in,
    qo_own, kv_own, qo_all, kv_all, kt_all, e_all, dp_all, ds_all, m_all, t_all, w_all,
    g_out, g_in, dq_out, dq_in,
    local, qo_send, qo_recv, kv_send, kv_recv, g_send, g_recv, dq_send, dq_recv,
):
    ctx = lax.axis_index("ctx")
    head = lax.axis_index("head")
    count = lax.axis_size("ctx")
    width, depth = kv_own.shape[1:]
    rows = qo_own.shape[2]
    group = rows // width
    slots = group * HEADS
    factor = depth ** -0.5

    def ctx_at(shift):
        return lax.rem(ctx + (shift + count), count)

    def head_at(shift):
        return lax.rem(head + (shift + HEADS), HEADS)

    def fetch(source, target, index):
        copy = pltpu.make_async_copy(source, target, local.at[index])
        copy.start()
        return copy

    def send(source, target, sems, index, ctx_shift=0, head_shift=0):
        copy = pltpu.make_async_remote_copy(
            src_ref=source, dst_ref=target, send_sem=sems[0].at[index], recv_sem=sems[1].at[index],
            device_id={"ctx": ctx_at(ctx_shift), "head": head_at(head_shift)}, device_id_type=MESH,
        )
        copy.start()
        return copy

    k_copy = fetch(k_hbm, k_in, 0)
    v_copy = fetch(v_hbm, v_in, 1)
    barrier = pltpu.get_barrier_semaphore()
    for s in range(1, SPAN):
        pl.semaphore_signal(
            barrier, inc=1, device_id={"ctx": ctx_at(-s), "head": head}, device_id_type=MESH
        )
    for k in range(1, HEADS):
        pl.semaphore_signal(
            barrier, inc=1, device_id={"ctx": ctx, "head": head_at(k)}, device_id_type=MESH
        )
    q_copy = fetch(q_hbm, q_in, 2)
    o_copy = fetch(o_hbm, o_in, 3)
    len_copy = fetch(len_hbm, len_in, 4)

    part = 2 * width
    tokens = part // HEADS
    pick = one_hot((tokens, part), lambda t: t * HEADS + head)
    k_copy.wait()
    v_copy.wait()
    for i in range(width // tokens):
        both = jnp.concatenate([k_in[i * part:(i + 1) * part], v_in[i * part:(i + 1) * part]], axis=1)
        both = jnp.dot(pick, both, preferred_element_type=F32).astype(BF16)
        kv_own[0, i * tokens:(i + 1) * tokens] = both[:, :depth]
        kv_own[1, i * tokens:(i + 1) * tokens] = both[:, depth:]

    pl.semaphore_wait(barrier, SPAN - 1 + HEADS - 1)
    kv_copies = [
        send(kv_own, kv_all.at[s - 1], (kv_send, kv_recv), s - 1, ctx_shift=s) for s in (3, 2, 1)
    ][::-1]

    tokens = part // slots
    order = one_hot((part, part), lambda r: lax.rem(r, tokens) * slots
                    + lax.rem(lax.div(r, tokens), group) * HEADS + lax.div(r, tokens * group))
    q_copy.wait()
    o_copy.wait()
    for i in range(width // tokens):
        both = jnp.concatenate([q_in[i * part:(i + 1) * part], o_in[i * part:(i + 1) * part]], axis=1)
        both = jnp.dot(order, both, preferred_element_type=F32).astype(BF16)
        for a in range(slots):
            g, j = divmod(a, group)
            here = slice(j * width + i * tokens, j * width + (i + 1) * tokens)
            qo_own[g, 0, here] = both[a * tokens:(a + 1) * tokens, :depth]
            qo_own[g, 1, here] = both[a * tokens:(a + 1) * tokens, depth:]
    qo_copies = [
        send(qo_own.at[head_at(k)], qo_all.at[k - 1], (qo_send, qo_recv), k - 1, head_shift=k)
        for k in range(1, HEADS)
    ]

    len_copy.wait()
    down = lax.broadcasted_iota(I32, (width, width), 0)
    across = lax.broadcasted_iota(I32, (width, width), 1)
    spread = jnp.broadcast_to(len_in[...], (width, width)).astype(F32)
    ends = jnp.sum(jnp.where(across <= down, spread, 0.0), axis=1, keepdims=True)
    own = jnp.sum(jnp.where(across == down, spread, 0.0), axis=1, keepdims=True)
    query_pos = ctx * width + across
    start = jnp.sum(
        jnp.where(ends <= query_pos.astype(F32), own, 0.0), axis=0, keepdims=True
    ).astype(I32)

    def qo(k):
        return qo_own.at[head] if k == 0 else qo_all.at[k - 1]

    def kv(s):
        return kv_own if s == 0 else kv_all.at[s - 1]

    scale = factor * LOG2E
    for s in range(SPAN):
        if s:
            kv_copies[s - 1].wait_recv()
        keys = kv(s)[0]
        values = kv(s)[1]
        kt_all[:, s * width:(s + 1) * width] = keys.T
        key_pos = (ctx - s) * width + down
        allowed = (key_pos >= start) & (key_pos <= query_pos)
        bias = jnp.where(allowed, 0.0, LOWEST)
        bias = jnp.concatenate([bias] * group, axis=1)
        for k in range(HEADS):
            if s == 0 and k:
                qo_copies[k - 1].wait_recv()
            cols = slice(k * rows, (k + 1) * rows)
            score = lax.dot_general(keys, qo(k)[0], NT, preferred_element_type=F32) + bias
            dprob = lax.dot_general(values, qo(k)[1], NT, preferred_element_type=F32)
            peak = jnp.max(score, axis=0, keepdims=True)
            expo = jnp.exp2((score - peak) * scale)
            m_all[s, :, cols] = peak
            t_all[s, :, cols] = jnp.sum(expo, axis=0, keepdims=True)
            w_all[s, :, cols] = jnp.sum(expo * dprob, axis=0, keepdims=True)
            e_all[s, :, cols] = expo
            dp_all[s, :, cols] = dprob

    peaks = [m_all[s] for s in range(SPAN)]
    peak = jnp.maximum(jnp.maximum(peaks[0], peaks[1]), jnp.maximum(peaks[2], peaks[3]))
    shares = [jnp.exp2((p - peak) * scale) for p in peaks]
    total = sum(t_all[s] * shares[s] for s in range(SPAN))
    inverse = 1.0 / total
    delta = sum(w_all[s] * shares[s] for s in range(SPAN)) * inverse
    shares = [share * inverse for share in shares]

    g_copies = []
    mine = None
    for s in (1, 2, 3, 0):
        keys_part = jnp.zeros((width, depth), F32)
        values_part = jnp.zeros((width, depth), F32)
        for k in range(HEADS):
            cols = slice(k * rows, (k + 1) * rows)
            prob = e_all[s, :, cols] * shares[s][:, cols]
            dscore = (prob * (dp_all[s, :, cols] - delta[:, cols])).astype(BF16)
            ds_all[s * width:(s + 1) * width, cols] = dscore
            keys_part += jnp.dot(dscore, qo(k)[0], preferred_element_type=F32)
            values_part += jnp.dot(prob.astype(BF16), qo(k)[1], preferred_element_type=F32)
        keys_part = keys_part * factor
        if s:
            g_out[s - 1, 0] = keys_part.astype(BF16)
            g_out[s - 1, 1] = values_part.astype(BF16)
            g_copies.append(send(g_out.at[s - 1], g_in.at[s - 1], (g_send, g_recv), s - 1, ctx_shift=-s))
        else:
            mine = (keys_part, values_part)

    dq_copies = []
    for k in (1, 2, 3, 0):
        cols = slice(k * rows, (k + 1) * rows)
        dq = jnp.dot(kt_all[...], ds_all[:, cols], preferred_element_type=F32)
        dq = (dq.T * factor).astype(BF16)
        if k:
            dq_out[k - 1] = dq
            dq_copies.append(
                send(dq_out.at[k - 1], dq_in.at[head], (dq_send, dq_recv), k - 1, head_shift=-k)
            )
        else:
            dq_in[head] = dq

    back = one_hot((part, part), lambda r: (lax.rem(r, HEADS) * group
                   + lax.rem(lax.div(r, HEADS), group)) * tokens + lax.div(r, slots))
    for k in range(1, HEADS):
        pltpu.make_async_remote_copy(
            src_ref=dq_out.at[k - 1], dst_ref=dq_in.at[head_at(k)],
            send_sem=dq_send.at[k - 1], recv_sem=dq_recv.at[k - 1],
            device_id={"ctx": ctx, "head": head_at(-k)}, device_id_type=MESH,
        ).wait_recv()
    for i in range(width // tokens):
        pieces = []
        for a in range(slots):
            g, j = divmod(a, group)
            pieces.append(dq_in[g, j * width + i * tokens:j * width + (i + 1) * tokens])
        dq_ref[i * part:(i + 1) * part] = jnp.dot(
            back, jnp.concatenate(pieces, axis=0), preferred_element_type=F32
        ).astype(BF16)

    for copy in g_copies:
        copy.wait_recv()
    for i, ref in enumerate((dk_ref, dv_ref)):
        acc = mine[i]
        for s in range(1, SPAN):
            acc = acc + g_in[s - 1, i].astype(F32)
        ref[...] = acc.astype(BF16)
    for copy in kv_copies + qo_copies + g_copies + dq_copies:
        copy.wait_send()


def on_device(queries, keys, values, out_grad, lengths):
    width, group, heads, depth = queries.shape
    rows = group * width
    total_q = heads * rows
    hbm = pl.BlockSpec(memory_space=pltpu.HBM)
    vmem = pl.BlockSpec(memory_space=pltpu.VMEM)
    dma = pltpu.SemaphoreType.DMA((3,))
    dq, dk, dv = pl.pallas_call(
        kernel,
        out_shape=(
            jax.ShapeDtypeStruct((total_q, depth), BF16),
            jax.ShapeDtypeStruct((width, depth), BF16),
            jax.ShapeDtypeStruct((width, depth), BF16),
        ),
        in_specs=[hbm] * 5,
        out_specs=(vmem, vmem, vmem),
        scratch_shapes=[
            pltpu.VMEM((1, lengths.shape[0]), I32),
            pltpu.VMEM((total_q, depth), BF16),
            pltpu.VMEM((heads * width, depth), BF16),
            pltpu.VMEM((heads * width, depth), BF16),
            pltpu.VMEM((total_q, depth), BF16),
            pltpu.VMEM((heads, 2, rows, depth), BF16),
            pltpu.VMEM((2, width, depth), BF16),
            pltpu.VMEM((HEADS - 1, 2, rows, depth), BF16),
            pltpu.VMEM((SPAN - 1, 2, width, depth), BF16),
            pltpu.VMEM((depth, SPAN * width), BF16),
            pltpu.VMEM((SPAN, width, total_q), F32),
            pltpu.VMEM((SPAN, width, total_q), F32),
            pltpu.VMEM((SPAN * width, total_q), BF16),
            pltpu.VMEM((SPAN, 1, total_q), F32),
            pltpu.VMEM((SPAN, 1, total_q), F32),
            pltpu.VMEM((SPAN, 1, total_q), F32),
            pltpu.VMEM((SPAN - 1, 2, width, depth), BF16),
            pltpu.VMEM((SPAN - 1, 2, width, depth), BF16),
            pltpu.VMEM((HEADS - 1, rows, depth), BF16),
            pltpu.VMEM((HEADS, rows, depth), BF16),
            pltpu.SemaphoreType.DMA((5,)),
        ] + [dma] * 8,
        compiler_params=pltpu.CompilerParams(
            collective_id=0, has_side_effects=True, vmem_limit_bytes=62 * 2 ** 20
        ),
    )(
        lengths.reshape(1, -1),
        queries.reshape(total_q, depth),
        keys.reshape(heads * width, depth),
        values.reshape(heads * width, depth),
        out_grad.reshape(total_q, depth),
    )
    return dq.reshape(queries.shape), dk[:, None, :], dv[:, None, :]


def solution(mesh):
    in_specs = (
        P("ctx", "head", None, None),
        P("ctx", None, None),
        P("ctx", None, None),
        P("ctx", "head", None, None),
        P(),
    )
    out_specs = (P("ctx", "head", None, None), P("ctx", "head", None), P("ctx", "head", None))
    return jax.shard_map(
        on_device, mesh=mesh, in_specs=in_specs, out_specs=out_specs, check_vma=False
    )
```

```python
import jax
import jax.numpy as jnp
from jax import lax
from jax.experimental import pallas as pl
from jax.experimental.pallas import tpu as pltpu
from jax.sharding import PartitionSpec as P

SPAN = 4
HEADS = 4
LOWEST = -1e30
LOG2E = 1.4426950408889634
MESH = pl.DeviceIdType.MESH
NT = (((1,), (1,)), ((), ()))
BF16, F32, I32 = jnp.bfloat16, jnp.float32, jnp.int32


def one_hot(shape, column_of_row):
    row = lax.broadcasted_iota(I32, shape, 0)
    column = lax.broadcasted_iota(I32, shape, 1)
    return jnp.where(column == column_of_row(row), 1.0, 0.0).astype(BF16)


def kernel(
    len_hbm, q_hbm, k_hbm, v_hbm, o_hbm,
    dq_ref, dkv_ref,
    len_in, q_in, k_in, v_in, o_in,
    qo_own, kv_own, qo_all, kv_all, kt_all, e_all, dp_all, ds_all, m_all, t_all, w_all,
    g_out, g_in, dq_out, dq_in,
    local, qo_send, qo_recv, kv_send, kv_recv, g_send, g_recv, dq_send, dq_recv,
):
    ctx = lax.axis_index("ctx")
    head = lax.axis_index("head")
    count = lax.axis_size("ctx")
    width, depth = kv_own.shape[1:]
    rows = qo_own.shape[2]
    group = rows // width
    slots = group * HEADS
    factor = depth ** -0.5

    def ctx_at(shift):
        return lax.rem(ctx + (shift + count), count)

    def head_at(shift):
        return lax.rem(head + (shift + HEADS), HEADS)

    def fetch(source, target, index):
        copy = pltpu.make_async_copy(source, target, local.at[index])
        copy.start()
        return copy

    def remote(source, target, sems, index, ctx_shift=0, head_shift=0):
        return pltpu.make_async_remote_copy(
            src_ref=source, dst_ref=target, send_sem=sems[0].at[index], recv_sem=sems[1].at[index],
            device_id={"ctx": ctx_at(ctx_shift), "head": head_at(head_shift)}, device_id_type=MESH,
        )

    def send(*args, **kwargs):
        copy = remote(*args, **kwargs)
        copy.start()
        return copy

    def later(s):
        return pl.when(ctx + s < count)

    def earlier(s):
        return pl.when(ctx >= s)

    k_copy = fetch(k_hbm, k_in, 0)
    v_copy = fetch(v_hbm, v_in, 1)
    barrier = pltpu.get_barrier_semaphore()
    for s in range(1, SPAN):
        @earlier(s)
        def _(s=s):
            pl.semaphore_signal(
                barrier, inc=1, device_id={"ctx": ctx_at(-s), "head": head}, device_id_type=MESH
            )
    for k in range(1, HEADS):
        pl.semaphore_signal(
            barrier, inc=1, device_id={"ctx": ctx, "head": head_at(k)}, device_id_type=MESH
        )
    q_copy = fetch(q_hbm, q_in, 2)
    o_copy = fetch(o_hbm, o_in, 3)
    len_copy = fetch(len_hbm, len_in, 4)

    part = 2 * width
    tokens = part // HEADS
    pick = one_hot((tokens, part), lambda t: t * HEADS + head)
    k_copy.wait()
    v_copy.wait()
    for i in range(width // tokens):
        both = jnp.concatenate([k_in[i * part:(i + 1) * part], v_in[i * part:(i + 1) * part]], axis=1)
        both = jnp.dot(pick, both, preferred_element_type=F32).astype(BF16)
        kv_own[0, i * tokens:(i + 1) * tokens] = both[:, :depth]
        kv_own[1, i * tokens:(i + 1) * tokens] = both[:, depth:]

    for s in range(SPAN):
        @pl.when(ctx + s < count if s == SPAN - 1 else ctx + s == count - 1)
        def _(s=s):
            pl.semaphore_wait(barrier, HEADS - 1 + s)

    for s in range(1, SPAN):
        @pl.when(ctx < s)
        def _(s=s):
            kv_all[s - 1] = jnp.zeros((2, width, depth), BF16)

        @pl.when(ctx + s >= count)
        def _(s=s):
            g_in[s - 1] = jnp.zeros((2, width, depth), BF16)

    kv_copies = [
        remote(kv_own, kv_all.at[s - 1], (kv_send, kv_recv), s - 1, ctx_shift=s) for s in range(1, SPAN)
    ]
    g_copies = [
        remote(g_out.at[s - 1], g_in.at[s - 1], (g_send, g_recv), s - 1, ctx_shift=-s)
        for s in range(1, SPAN)
    ]
    for s in (1, 2, 3):
        later(s)(kv_copies[s - 1].start)

    tokens = part // slots
    order = one_hot((part, part), lambda r: lax.rem(r, tokens) * slots
                    + lax.rem(lax.div(r, tokens), group) * HEADS + lax.div(r, tokens * group))
    q_copy.wait()
    o_copy.wait()
    for i in range(width // tokens):
        both = jnp.concatenate([q_in[i * part:(i + 1) * part], o_in[i * part:(i + 1) * part]], axis=1)
        both = jnp.dot(order, both, preferred_element_type=F32).astype(BF16)
        for a in range(slots):
            g, j = divmod(a, group)
            here = slice(j * width + i * tokens, j * width + (i + 1) * tokens)
            qo_own[g, 0, here] = both[a * tokens:(a + 1) * tokens, :depth]
            qo_own[g, 1, here] = both[a * tokens:(a + 1) * tokens, depth:]
    qo_copies = [
        send(qo_own.at[head_at(k)], qo_all.at[k - 1], (qo_send, qo_recv), k - 1, head_shift=k)
        for k in range(1, HEADS)
    ]

    len_copy.wait()
    down = lax.broadcasted_iota(I32, (width, width), 0)
    across = lax.broadcasted_iota(I32, (width, width), 1)
    spread = jnp.broadcast_to(len_in[...], (width, width)).astype(F32)
    ends = jnp.sum(jnp.where(across <= down, spread, 0.0), axis=1, keepdims=True)
    own = jnp.sum(jnp.where(across == down, spread, 0.0), axis=1, keepdims=True)
    query_pos = ctx * width + across
    start = jnp.sum(
        jnp.where(ends <= query_pos.astype(F32), own, 0.0), axis=0, keepdims=True
    ).astype(I32)


    def qo(k):
        return qo_own.at[head] if k == 0 else qo_all.at[k - 1]

    def kv(s):
        return kv_own if s == 0 else kv_all.at[s - 1]

    scale = factor * LOG2E
    for s in range(SPAN):
        if s:
            earlier(s)(kv_copies[s - 1].wait_recv)
        keys = kv(s)[0]
        values = kv(s)[1]
        kt_all[:, s * width:(s + 1) * width] = keys.T
        key_pos = (ctx - s) * width + down
        allowed = (key_pos >= start) & (key_pos <= query_pos)
        bias = jnp.where(allowed, 0.0, LOWEST)
        bias = jnp.concatenate([bias] * group, axis=1)
        for k in range(HEADS):
            if s == 0 and k:
                qo_copies[k - 1].wait_recv()
            cols = slice(k * rows, (k + 1) * rows)
            score = lax.dot_general(keys, qo(k)[0], NT, preferred_element_type=F32) + bias
            dprob = lax.dot_general(values, qo(k)[1], NT, preferred_element_type=F32)
            peak = jnp.max(score, axis=0, keepdims=True)
            expo = jnp.exp2((score - peak) * scale)
            m_all[s, :, cols] = peak
            t_all[s, :, cols] = jnp.sum(expo, axis=0, keepdims=True)
            w_all[s, :, cols] = jnp.sum(expo * dprob, axis=0, keepdims=True)
            e_all[s, :, cols] = expo
            dp_all[s, :, cols] = dprob

    peaks = [m_all[s] for s in range(SPAN)]
    peak = jnp.maximum(jnp.maximum(peaks[0], peaks[1]), jnp.maximum(peaks[2], peaks[3]))
    shares = [jnp.exp2((p - peak) * scale) for p in peaks]
    total = sum(t_all[s] * shares[s] for s in range(SPAN))
    inverse = 1.0 / total
    delta = sum(w_all[s] * shares[s] for s in range(SPAN)) * inverse
    shares = [share * inverse for share in shares]

    mine = None
    for s in (1, 2, 3, 0):
        keys_part = jnp.zeros((width, depth), F32)
        values_part = jnp.zeros((width, depth), F32)
        for k in range(HEADS):
            cols = slice(k * rows, (k + 1) * rows)
            prob = e_all[s, :, cols] * shares[s][:, cols]
            dscore = (prob * (dp_all[s, :, cols] - delta[:, cols])).astype(BF16)
            ds_all[s * width:(s + 1) * width, cols] = dscore
            keys_part += jnp.dot(dscore, qo(k)[0], preferred_element_type=F32)
            values_part += jnp.dot(prob.astype(BF16), qo(k)[1], preferred_element_type=F32)
        keys_part = keys_part * factor
        if s:
            g_out[s - 1, 0] = keys_part.astype(BF16)
            g_out[s - 1, 1] = values_part.astype(BF16)
            earlier(s)(g_copies[s - 1].start)
        else:
            mine = (keys_part, values_part)

    dq_copies = []
    for k in (1, 2, 3, 0):
        cols = slice(k * rows, (k + 1) * rows)
        dq = jnp.dot(kt_all[...], ds_all[:, cols], preferred_element_type=F32)
        dq = (dq.T * factor).astype(BF16)
        if k:
            dq_out[k - 1] = dq
            dq_copies.append(
                send(dq_out.at[k - 1], dq_in.at[head], (dq_send, dq_recv), k - 1, head_shift=-k)
            )
        else:
            dq_in[head] = dq


    back = one_hot((part, part), lambda r: (lax.rem(r, HEADS) * group
                   + lax.rem(lax.div(r, HEADS), group)) * tokens + lax.div(r, slots))
    for k in range(1, HEADS):
        pltpu.make_async_remote_copy(
            src_ref=dq_out.at[k - 1], dst_ref=dq_in.at[head_at(k)],
            send_sem=dq_send.at[k - 1], recv_sem=dq_recv.at[k - 1],
            device_id={"ctx": ctx, "head": head_at(-k)}, device_id_type=MESH,
        ).wait_recv()
    for i in range(width // tokens):
        pieces = []
        for a in range(slots):
            g, j = divmod(a, group)
            pieces.append(dq_in[g, j * width + i * tokens:j * width + (i + 1) * tokens])
        dq_ref[i * part:(i + 1) * part] = jnp.dot(
            back, jnp.concatenate(pieces, axis=0), preferred_element_type=F32
        ).astype(BF16)

    for s in range(1, SPAN):
        later(s)(g_copies[s - 1].wait_recv)
    for i in range(2):
        acc = mine[i]
        for s in range(1, SPAN):
            acc = acc + g_in[s - 1, i].astype(F32)
        dkv_ref[i] = acc.astype(BF16)
    for s in range(1, SPAN):
        later(s)(kv_copies[s - 1].wait_send)
        earlier(s)(g_copies[s - 1].wait_send)
    for copy in qo_copies + dq_copies:
        copy.wait_send()


def on_device(queries, keys, values, out_grad, lengths):
    width, group, heads, depth = queries.shape
    rows = group * width
    total_q = heads * rows
    hbm = pl.BlockSpec(memory_space=pltpu.HBM)
    vmem = pl.BlockSpec(memory_space=pltpu.VMEM)
    dma = pltpu.SemaphoreType.DMA((3,))
    dq, dkv = pl.pallas_call(
        kernel,
        out_shape=(
            pltpu.VMEM((total_q, depth), BF16),
            pltpu.VMEM((2, width, depth), BF16),
        ),
        in_specs=[hbm] * 5,
        out_specs=(vmem, vmem),
        scratch_shapes=[
            pltpu.VMEM((1, lengths.shape[0]), I32),
            pltpu.VMEM((total_q, depth), BF16),
            pltpu.VMEM((heads * width, depth), BF16),
            pltpu.VMEM((heads * width, depth), BF16),
            pltpu.VMEM((total_q, depth), BF16),
            pltpu.VMEM((heads, 2, rows, depth), BF16),
            pltpu.VMEM((2, width, depth), BF16),
            pltpu.VMEM((HEADS - 1, 2, rows, depth), BF16),
            pltpu.VMEM((SPAN - 1, 2, width, depth), BF16),
            pltpu.VMEM((depth, SPAN * width), BF16),
            pltpu.VMEM((SPAN, width, total_q), F32),
            pltpu.VMEM((SPAN, width, total_q), F32),
            pltpu.VMEM((SPAN * width, total_q), BF16),
            pltpu.VMEM((SPAN, 1, total_q), F32),
            pltpu.VMEM((SPAN, 1, total_q), F32),
            pltpu.VMEM((SPAN, 1, total_q), F32),
            pltpu.VMEM((SPAN - 1, 2, width, depth), BF16),
            pltpu.VMEM((SPAN - 1, 2, width, depth), BF16),
            pltpu.VMEM((HEADS - 1, rows, depth), BF16),
            pltpu.VMEM((HEADS, rows, depth), BF16),
            pltpu.SemaphoreType.DMA((5,)),
        ] + [dma] * 8,
        compiler_params=pltpu.CompilerParams(
            collective_id=0, has_side_effects=True, vmem_limit_bytes=62 * 2 ** 20
        ),
    )(
        lengths.reshape(1, -1),
        queries.reshape(total_q, depth),
        keys.reshape(heads * width, depth),
        values.reshape(heads * width, depth),
        out_grad.reshape(total_q, depth),
    )
    return dq.reshape(queries.shape), dkv[0][:, None, :], dkv[1][:, None, :]


def solution(mesh):
    in_specs = (
        P("ctx", "head", None, None),
        P("ctx", None, None),
        P("ctx", None, None),
        P("ctx", "head", None, None),
        P(),
    )
    out_specs = (P("ctx", "head", None, None), P("ctx", "head", None), P("ctx", "head", None))
    return jax.shard_map(
        on_device, mesh=mesh, in_specs=in_specs, out_specs=out_specs, check_vma=False
    )
```

```python
import jax
import jax.numpy as jnp
from jax import lax
from jax.experimental import pallas as pl
from jax.experimental.pallas import tpu as pltpu
from jax.sharding import PartitionSpec as P

SPAN = 4
ROW = 16
HEADS = 4
LOWEST = -1e30
LOG2E = 1.4426950408889634
MESH = pl.DeviceIdType.MESH
NT = (((1,), (1,)), ((), ()))
BF16, F32, I32 = jnp.bfloat16, jnp.float32, jnp.int32


def one_hot(shape, column_of_row):
    row = lax.broadcasted_iota(I32, shape, 0)
    column = lax.broadcasted_iota(I32, shape, 1)
    return jnp.where(column == column_of_row(row), 1.0, 0.0).astype(BF16)


def kernel(
    len_hbm, q_hbm, k_hbm, v_hbm, o_hbm,
    dq_ref, dkv_ref,
    len_in, q_in, k_in, v_in, o_in,
    qo_own, kv_own, qo_all, kv_all, kt_all, e_all, dp_all, ds_all, m_all, t_all, w_all,
    g_out, g_in, dq_out, dq_in,
    local, qo_send, qo_recv, kv_send, kv_recv, g_send, g_recv, dq_send, dq_recv,
):
    ctx = lax.axis_index("ctx")
    head = lax.axis_index("head")
    count = lax.axis_size("ctx")
    place = lax.rem(ctx, ROW)
    width, depth = kv_own.shape[1:]
    rows = qo_own.shape[2]
    group = rows // width
    slots = group * HEADS
    factor = depth ** -0.5

    def ctx_at(shift):
        return lax.rem(ctx + (shift + count), count)

    def head_at(shift):
        return lax.rem(head + (shift + HEADS), HEADS)

    def fetch(source, target, index):
        copy = pltpu.make_async_copy(source, target, local.at[index])
        copy.start()
        return copy

    def remote(source, target, sems, index, ctx_shift=0, head_shift=0):
        return pltpu.make_async_remote_copy(
            src_ref=source, dst_ref=target, send_sem=sems[0].at[index], recv_sem=sems[1].at[index],
            device_id={"ctx": ctx_at(ctx_shift), "head": head_at(head_shift)}, device_id_type=MESH,
        )

    def send(*args, **kwargs):
        copy = remote(*args, **kwargs)
        copy.start()
        return copy

    def later(s):
        return pl.when(ctx + s < count)

    def earlier(s):
        return pl.when(ctx >= s)

    k_copy = fetch(k_hbm, k_in, 0)
    v_copy = fetch(v_hbm, v_in, 1)
    barrier = pltpu.get_barrier_semaphore()
    for s in range(1, SPAN):
        @earlier(s)
        def _(s=s):
            pl.semaphore_signal(
                barrier, inc=1, device_id={"ctx": ctx_at(-s), "head": head}, device_id_type=MESH
            )
    for k in range(1, HEADS):
        pl.semaphore_signal(
            barrier, inc=1, device_id={"ctx": ctx, "head": head_at(k)}, device_id_type=MESH
        )
    q_copy = fetch(q_hbm, q_in, 2)
    o_copy = fetch(o_hbm, o_in, 3)
    len_copy = fetch(len_hbm, len_in, 4)

    part = 2 * width
    tokens = part // HEADS
    pick = one_hot((tokens, part), lambda t: t * HEADS + head)
    k_copy.wait()
    v_copy.wait()
    for i in range(width // tokens):
        both = jnp.concatenate([k_in[i * part:(i + 1) * part], v_in[i * part:(i + 1) * part]], axis=1)
        both = jnp.dot(pick, both, preferred_element_type=F32).astype(BF16)
        kv_own[0, i * tokens:(i + 1) * tokens] = both[:, :depth]
        kv_own[1, i * tokens:(i + 1) * tokens] = both[:, depth:]

    for s in range(SPAN):
        @pl.when(ctx + s < count if s == SPAN - 1 else ctx + s == count - 1)
        def _(s=s):
            pl.semaphore_wait(barrier, HEADS - 1 + s)

    for s in range(1, SPAN):
        @pl.when(ctx < s)
        def _(s=s):
            kv_all[s - 1] = jnp.zeros((2, width, depth), BF16)

        @pl.when(ctx + s >= count)
        def _(s=s):
            g_in[s - 1] = jnp.zeros((2, width, depth), BF16)

    kv_copies = [
        remote(kv_own, kv_all.at[s - 1], (kv_send, kv_recv), s - 1, ctx_shift=s) for s in range(1, SPAN)
    ]
    g_copies = [
        remote(g_out.at[s - 1], g_in.at[s - 1], (g_send, g_recv), s - 1, ctx_shift=-s)
        for s in range(1, SPAN)
    ]
    for s in (1, 2, 3):
        later(s)(kv_copies[s - 1].start)

    tokens = part // slots
    order = one_hot((part, part), lambda r: lax.rem(r, tokens) * slots
                    + lax.rem(lax.div(r, tokens), group) * HEADS + lax.div(r, tokens * group))
    q_copy.wait()
    o_copy.wait()
    for i in range(width // tokens):
        both = jnp.concatenate([q_in[i * part:(i + 1) * part], o_in[i * part:(i + 1) * part]], axis=1)
        both = jnp.dot(order, both, preferred_element_type=F32).astype(BF16)
        for a in range(slots):
            g, j = divmod(a, group)
            here = slice(j * width + i * tokens, j * width + (i + 1) * tokens)
            qo_own[g, 0, here] = both[a * tokens:(a + 1) * tokens, :depth]
            qo_own[g, 1, here] = both[a * tokens:(a + 1) * tokens, depth:]
    qo_copies = [
        send(qo_own.at[head_at(k)], qo_all.at[k - 1], (qo_send, qo_recv), k - 1, head_shift=k)
        for k in range(1, HEADS)
    ]

    len_copy.wait()
    down = lax.broadcasted_iota(I32, (width, width), 0)
    across = lax.broadcasted_iota(I32, (width, width), 1)
    spread = jnp.broadcast_to(len_in[...], (width, width)).astype(F32)
    ends = jnp.sum(jnp.where(across <= down, spread, 0.0), axis=1, keepdims=True)
    own = jnp.sum(jnp.where(across == down, spread, 0.0), axis=1, keepdims=True)
    query_pos = ctx * width + across
    start = jnp.sum(
        jnp.where(ends <= query_pos.astype(F32), own, 0.0), axis=0, keepdims=True
    ).astype(I32)


    def qo(k):
        return qo_own.at[head] if k == 0 else qo_all.at[k - 1]

    def kv(s):
        return kv_own if s == 0 else kv_all.at[s - 1]

    scale = factor * LOG2E
    for s in range(SPAN):
        if s:
            earlier(s)(kv_copies[s - 1].wait_recv)
        keys = kv(s)[0]
        values = kv(s)[1]
        kt_all[:, s * width:(s + 1) * width] = keys.T
        key_pos = (ctx - s) * width + down
        allowed = (key_pos >= start) & (key_pos <= query_pos)
        bias = jnp.where(allowed, 0.0, LOWEST)
        bias = jnp.concatenate([bias] * group, axis=1)
        for k in range(HEADS):
            if s == 0 and k:
                qo_copies[k - 1].wait_recv()
            cols = slice(k * rows, (k + 1) * rows)
            score = lax.dot_general(keys, qo(k)[0], NT, preferred_element_type=F32) + bias
            dprob = lax.dot_general(values, qo(k)[1], NT, preferred_element_type=F32)
            peak = jnp.max(score, axis=0, keepdims=True)
            expo = jnp.exp2((score - peak) * scale)
            m_all[s, :, cols] = peak
            t_all[s, :, cols] = jnp.sum(expo, axis=0, keepdims=True)
            w_all[s, :, cols] = jnp.sum(expo * dprob, axis=0, keepdims=True)
            e_all[s, :, cols] = expo
            dp_all[s, :, cols] = dprob

    peaks = [m_all[s] for s in range(SPAN)]
    peak = jnp.maximum(jnp.maximum(peaks[0], peaks[1]), jnp.maximum(peaks[2], peaks[3]))
    shares = [jnp.exp2((p - peak) * scale) for p in peaks]
    total = sum(t_all[s] * shares[s] for s in range(SPAN))
    inverse = 1.0 / total
    delta = sum(w_all[s] * shares[s] for s in range(SPAN)) * inverse
    shares = [share * inverse for share in shares]

    mine = None
    for s in (1, 2, 3, 0):
        keys_part = jnp.zeros((width, depth), F32)
        values_part = jnp.zeros((width, depth), F32)
        for k in range(HEADS):
            cols = slice(k * rows, (k + 1) * rows)
            prob = e_all[s, :, cols] * shares[s][:, cols]
            dscore = (prob * (dp_all[s, :, cols] - delta[:, cols])).astype(BF16)
            ds_all[s * width:(s + 1) * width, cols] = dscore
            keys_part += jnp.dot(dscore, qo(k)[0], preferred_element_type=F32)
            values_part += jnp.dot(prob.astype(BF16), qo(k)[1], preferred_element_type=F32)
        keys_part = keys_part * factor
        if s:
            g_out[s - 1, 0] = keys_part.astype(BF16)
            g_out[s - 1, 1] = values_part.astype(BF16)
            pl.when((ctx >= s) & ((place == 0) | (place >= s)))(g_copies[s - 1].start)
        else:
            mine = (keys_part, values_part)

    dq_copies = []
    for k in (1, 2, 3, 0):
        cols = slice(k * rows, (k + 1) * rows)
        dq = jnp.dot(kt_all[...], ds_all[:, cols], preferred_element_type=F32)
        dq = (dq.T * factor).astype(BF16)
        if k:
            dq_out[k - 1] = dq
            dq_copies.append(
                send(dq_out.at[k - 1], dq_in.at[head], (dq_send, dq_recv), k - 1, head_shift=-k)
            )
        else:
            dq_in[head] = dq


    for s in range(2, SPAN):
        pl.when((place == 1) & (ctx >= s))(g_copies[s - 1].start)

    back = one_hot((part, part), lambda r: (lax.rem(r, HEADS) * group
                   + lax.rem(lax.div(r, HEADS), group)) * tokens + lax.div(r, slots))
    for k in range(1, HEADS):
        pltpu.make_async_remote_copy(
            src_ref=dq_out.at[k - 1], dst_ref=dq_in.at[head_at(k)],
            send_sem=dq_send.at[k - 1], recv_sem=dq_recv.at[k - 1],
            device_id={"ctx": ctx, "head": head_at(-k)}, device_id_type=MESH,
        ).wait_recv()
    pl.when((place == 2) & (ctx >= 3))(g_copies[2].start)
    for i in range(width // tokens):
        pieces = []
        for a in range(slots):
            g, j = divmod(a, group)
            pieces.append(dq_in[g, j * width + i * tokens:j * width + (i + 1) * tokens])
        dq_ref[i * part:(i + 1) * part] = jnp.dot(
            back, jnp.concatenate(pieces, axis=0), preferred_element_type=F32
        ).astype(BF16)

    for s in range(1, SPAN):
        later(s)(g_copies[s - 1].wait_recv)
    for i in range(2):
        acc = mine[i]
        for s in range(1, SPAN):
            acc = acc + g_in[s - 1, i].astype(F32)
        dkv_ref[i] = acc.astype(BF16)
    for s in range(1, SPAN):
        later(s)(kv_copies[s - 1].wait_send)
        earlier(s)(g_copies[s - 1].wait_send)
    for copy in qo_copies + dq_copies:
        copy.wait_send()


def store(dq_ref, dkv_ref, dq_hbm, dk_hbm, dv_hbm, sems):
    pairs = ((dq_ref, dq_hbm), (dkv_ref.at[0], dk_hbm), (dkv_ref.at[1], dv_hbm))
    copies = [pltpu.make_async_copy(a, b, sems.at[i]) for i, (a, b) in enumerate(pairs)]
    for copy in copies:
        copy.start()
    for copy in copies:
        copy.wait()


def on_device(queries, keys, values, out_grad, lengths):
    width, group, heads, depth = queries.shape
    rows = group * width
    total_q = heads * rows
    hbm = pl.BlockSpec(memory_space=pltpu.HBM)
    vmem = pl.BlockSpec(memory_space=pltpu.VMEM)
    dma = pltpu.SemaphoreType.DMA((3,))
    dq, dkv = pl.pallas_call(
        kernel,
        out_shape=(
            pltpu.VMEM((total_q, depth), BF16),
            pltpu.VMEM((2, width, depth), BF16),
        ),
        in_specs=[hbm] * 5,
        out_specs=(vmem, vmem),
        scratch_shapes=[
            pltpu.VMEM((1, lengths.shape[0]), I32),
            pltpu.VMEM((total_q, depth), BF16),
            pltpu.VMEM((heads * width, depth), BF16),
            pltpu.VMEM((heads * width, depth), BF16),
            pltpu.VMEM((total_q, depth), BF16),
            pltpu.VMEM((heads, 2, rows, depth), BF16),
            pltpu.VMEM((2, width, depth), BF16),
            pltpu.VMEM((HEADS - 1, 2, rows, depth), BF16),
            pltpu.VMEM((SPAN - 1, 2, width, depth), BF16),
            pltpu.VMEM((depth, SPAN * width), BF16),
            pltpu.VMEM((SPAN, width, total_q), F32),
            pltpu.VMEM((SPAN, width, total_q), F32),
            pltpu.VMEM((SPAN * width, total_q), BF16),
            pltpu.VMEM((SPAN, 1, total_q), F32),
            pltpu.VMEM((SPAN, 1, total_q), F32),
            pltpu.VMEM((SPAN, 1, total_q), F32),
            pltpu.VMEM((SPAN - 1, 2, width, depth), BF16),
            pltpu.VMEM((SPAN - 1, 2, width, depth), BF16),
            pltpu.VMEM((HEADS - 1, rows, depth), BF16),
            pltpu.VMEM((HEADS, rows, depth), BF16),
            pltpu.SemaphoreType.DMA((5,)),
        ] + [dma] * 8,
        compiler_params=pltpu.CompilerParams(
            collective_id=0, has_side_effects=True, vmem_limit_bytes=62 * 2 ** 20
        ),
    )(
        lengths.reshape(1, -1),
        queries.reshape(total_q, depth),
        keys.reshape(heads * width, depth),
        values.reshape(heads * width, depth),
        out_grad.reshape(total_q, depth),
    )
    vin = pl.BlockSpec(memory_space=pltpu.VMEM)
    dq, dk, dv = pl.pallas_call(
        store,
        out_shape=(
            jax.ShapeDtypeStruct((total_q, depth), BF16),
            jax.ShapeDtypeStruct((width, depth), BF16),
            jax.ShapeDtypeStruct((width, depth), BF16),
        ),
        in_specs=[pl.BlockSpec(memory_space=pl.ANY)] * 2,
        out_specs=(hbm, hbm, hbm),
        scratch_shapes=[pltpu.SemaphoreType.DMA((3,))],
        compiler_params=pltpu.CompilerParams(vmem_limit_bytes=4 * 2 ** 20),
    )(dq, dkv)
    return dq.reshape(queries.shape), dk[:, None, :], dv[:, None, :]


def solution(mesh):
    in_specs = (
        P("ctx", "head", None, None),
        P("ctx", None, None),
        P("ctx", None, None),
        P("ctx", "head", None, None),
        P(),
    )
    out_specs = (P("ctx", "head", None, None), P("ctx", "head", None), P("ctx", "head", None))
    return jax.shard_map(
        on_device, mesh=mesh, in_specs=in_specs, out_specs=out_specs, check_vma=False
    )
```

```python
import jax
import jax.numpy as jnp
from jax import lax
from jax.experimental import pallas as pl
from jax.experimental.pallas import tpu as pltpu
from jax.sharding import PartitionSpec as P

SPAN = 4
ROW = 16
HEADS = 4
LOWEST = -1e30
LOG2E = 1.4426950408889634
MESH = pl.DeviceIdType.MESH
NT = (((1,), (1,)), ((), ()))
BF16, F32, I32 = jnp.bfloat16, jnp.float32, jnp.int32


def one_hot(shape, column_of_row):
    row = lax.broadcasted_iota(I32, shape, 0)
    column = lax.broadcasted_iota(I32, shape, 1)
    return jnp.where(column == column_of_row(row), 1.0, 0.0).astype(BF16)


def kernel(
    len_hbm, q_hbm, k_hbm, v_hbm, o_hbm,
    dq_ref, dkv_ref,
    len_in, q_in, k_in, v_in, o_in,
    qo_own, kv_own, qo_all, kv_all, kt_all, e_all, dp_all, ds_all, m_all, t_all, w_all,
    g_out, g_in, dq_out, dq_in,
    local, qo_send, qo_recv, kv_send, relay_send, kv_recv, g_send, g_recv, dq_send, dq_recv,
):
    ctx = lax.axis_index("ctx")
    head = lax.axis_index("head")
    count = lax.axis_size("ctx")
    place = lax.rem(ctx, ROW)
    width, depth = kv_own.shape[1:]
    rows = qo_own.shape[2]
    group = rows // width
    slots = group * HEADS
    factor = depth ** -0.5

    def ctx_at(shift):
        return lax.rem(ctx + (shift + count), count)

    def head_at(shift):
        return lax.rem(head + (shift + HEADS), HEADS)

    def fetch(source, target, index):
        copy = pltpu.make_async_copy(source, target, local.at[index])
        copy.start()
        return copy

    def remote(source, target, sems, index, ctx_shift=0, head_shift=0):
        sender, receiver = index if isinstance(index, tuple) else (index, index)
        return pltpu.make_async_remote_copy(
            src_ref=source, dst_ref=target, send_sem=sems[0].at[sender], recv_sem=sems[1].at[receiver],
            device_id={"ctx": ctx_at(ctx_shift), "head": head_at(head_shift)}, device_id_type=MESH,
        )

    def send(*args, **kwargs):
        copy = remote(*args, **kwargs)
        copy.start()
        return copy

    def later(s):
        return pl.when(ctx + s < count)

    def earlier(s):
        return pl.when(ctx >= s)

    def direct(s):
        return (ctx + s < count) & ((place + s != ROW) | (s != 2))

    def relay():
        return pl.when((place == 1) & (ctx > ROW))

    k_copy = fetch(k_hbm, k_in, 0)
    v_copy = fetch(v_hbm, v_in, 1)
    barrier = pltpu.get_barrier_semaphore()
    for s in range(1, SPAN):
        @earlier(s)
        def _(s=s):
            pl.semaphore_signal(
                barrier, inc=1, device_id={"ctx": ctx_at(-s), "head": head}, device_id_type=MESH
            )
    for k in range(1, HEADS):
        pl.semaphore_signal(
            barrier, inc=1, device_id={"ctx": ctx, "head": head_at(k)}, device_id_type=MESH
        )
    q_copy = fetch(q_hbm, q_in, 2)
    o_copy = fetch(o_hbm, o_in, 3)
    len_copy = fetch(len_hbm, len_in, 4)

    part = 2 * width
    tokens = part // HEADS
    pick = one_hot((tokens, part), lambda t: t * HEADS + head)
    k_copy.wait()
    v_copy.wait()
    for i in range(width // tokens):
        both = jnp.concatenate([k_in[i * part:(i + 1) * part], v_in[i * part:(i + 1) * part]], axis=1)
        both = jnp.dot(pick, both, preferred_element_type=F32).astype(BF16)
        kv_own[0, i * tokens:(i + 1) * tokens] = both[:, :depth]
        kv_own[1, i * tokens:(i + 1) * tokens] = both[:, depth:]

    for s in range(SPAN):
        @pl.when(ctx + s < count if s == SPAN - 1 else ctx + s == count - 1)
        def _(s=s):
            pl.semaphore_wait(barrier, HEADS - 1 + s)

    for s in range(1, SPAN):
        @pl.when(ctx < s)
        def _(s=s):
            kv_all[s - 1] = jnp.zeros((2, width, depth), BF16)

        @pl.when(ctx + s >= count)
        def _(s=s):
            g_in[s - 1] = jnp.zeros((2, width, depth), BF16)

    kv_copies = [
        remote(kv_own, kv_all.at[s - 1], (kv_send, kv_recv), s - 1, ctx_shift=s) for s in range(1, SPAN)
    ]
    g_copies = [
        remote(g_out.at[s - 1], g_in.at[s - 1], (g_send, g_recv), s - 1, ctx_shift=-s)
        for s in range(1, SPAN)
    ]
    passed_on = remote(kv_all.at[2], kv_all.at[1], (relay_send, kv_recv), (0, 1), ctx_shift=-1)
    for s in (3, 1):
        pl.when(direct(s) & (place == ROW - 2))(kv_copies[s - 1].start)
    for s in (1, 2, 3):
        pl.when(direct(s) & (place == ROW - 3))(kv_copies[s - 1].start)
    for s in (1, 2, 3):
        pl.when(direct(s) & ((place < ROW - 3) | (place == ROW - 1)))(kv_copies[s - 1].start)

    tokens = part // slots
    order = one_hot((part, part), lambda r: lax.rem(r, tokens) * slots
                    + lax.rem(lax.div(r, tokens), group) * HEADS + lax.div(r, tokens * group))
    q_copy.wait()
    o_copy.wait()
    for i in range(width // tokens):
        both = jnp.concatenate([q_in[i * part:(i + 1) * part], o_in[i * part:(i + 1) * part]], axis=1)
        both = jnp.dot(order, both, preferred_element_type=F32).astype(BF16)
        for a in range(slots):
            g, j = divmod(a, group)
            here = slice(j * width + i * tokens, j * width + (i + 1) * tokens)
            qo_own[g, 0, here] = both[a * tokens:(a + 1) * tokens, :depth]
            qo_own[g, 1, here] = both[a * tokens:(a + 1) * tokens, depth:]
    qo_copies = [
        send(qo_own.at[head_at(k)], qo_all.at[k - 1], (qo_send, qo_recv), k - 1, head_shift=k)
        for k in range(1, HEADS)
    ]

    len_copy.wait()
    down = lax.broadcasted_iota(I32, (width, width), 0)
    across = lax.broadcasted_iota(I32, (width, width), 1)
    spread = jnp.broadcast_to(len_in[...], (width, width)).astype(F32)
    ends = jnp.sum(jnp.where(across <= down, spread, 0.0), axis=1, keepdims=True)
    own = jnp.sum(jnp.where(across == down, spread, 0.0), axis=1, keepdims=True)
    query_pos = ctx * width + across
    start = jnp.sum(
        jnp.where(ends <= query_pos.astype(F32), own, 0.0), axis=0, keepdims=True
    ).astype(I32)


    def qo(k):
        return qo_own.at[head] if k == 0 else qo_all.at[k - 1]

    def kv(s):
        return kv_own if s == 0 else kv_all.at[s - 1]

    scale = factor * LOG2E
    for s in (0, 1, 3, 2):
        if s:
            earlier(s)(kv_copies[s - 1].wait_recv)
            if s == 3:
                relay()(passed_on.start)
        keys = kv(s)[0]
        values = kv(s)[1]
        kt_all[:, s * width:(s + 1) * width] = keys.T
        key_pos = (ctx - s) * width + down
        allowed = (key_pos >= start) & (key_pos <= query_pos)
        bias = jnp.where(allowed, 0.0, LOWEST)
        bias = jnp.concatenate([bias] * group, axis=1)
        for k in range(HEADS):
            if s == 0 and k:
                qo_copies[k - 1].wait_recv()
            cols = slice(k * rows, (k + 1) * rows)
            score = lax.dot_general(keys, qo(k)[0], NT, preferred_element_type=F32) + bias
            dprob = lax.dot_general(values, qo(k)[1], NT, preferred_element_type=F32)
            peak = jnp.max(score, axis=0, keepdims=True)
            expo = jnp.exp2((score - peak) * scale)
            m_all[s, :, cols] = peak
            t_all[s, :, cols] = jnp.sum(expo, axis=0, keepdims=True)
            w_all[s, :, cols] = jnp.sum(expo * dprob, axis=0, keepdims=True)
            e_all[s, :, cols] = expo
            dp_all[s, :, cols] = dprob

    peaks = [m_all[s] for s in range(SPAN)]
    peak = jnp.maximum(jnp.maximum(peaks[0], peaks[1]), jnp.maximum(peaks[2], peaks[3]))
    shares = [jnp.exp2((p - peak) * scale) for p in peaks]
    total = sum(t_all[s] * shares[s] for s in range(SPAN))
    inverse = 1.0 / total
    delta = sum(w_all[s] * shares[s] for s in range(SPAN)) * inverse
    shares = [share * inverse for share in shares]

    mine = None
    for s in (1, 2, 3, 0):
        keys_part = jnp.zeros((width, depth), F32)
        values_part = jnp.zeros((width, depth), F32)
        for k in range(HEADS):
            cols = slice(k * rows, (k + 1) * rows)
            prob = e_all[s, :, cols] * shares[s][:, cols]
            dscore = (prob * (dp_all[s, :, cols] - delta[:, cols])).astype(BF16)
            ds_all[s * width:(s + 1) * width, cols] = dscore
            keys_part += jnp.dot(dscore, qo(k)[0], preferred_element_type=F32)
            values_part += jnp.dot(prob.astype(BF16), qo(k)[1], preferred_element_type=F32)
        keys_part = keys_part * factor
        if s:
            g_out[s - 1, 0] = keys_part.astype(BF16)
            g_out[s - 1, 1] = values_part.astype(BF16)
            pl.when((ctx >= s) & ((place == 0) | (place >= s)))(g_copies[s - 1].start)
        else:
            mine = (keys_part, values_part)

    dq_copies = []
    for k in (2, 1, 3, 0):
        cols = slice(k * rows, (k + 1) * rows)
        dq = jnp.dot(kt_all[...], ds_all[:, cols], preferred_element_type=F32)
        dq = (dq.T * factor).astype(BF16)
        if k:
            dq_out[k - 1] = dq
            dq_copies.append(
                send(dq_out.at[k - 1], dq_in.at[head], (dq_send, dq_recv), k - 1, head_shift=-k)
            )
        else:
            dq_in[head] = dq


    for s in range(2, SPAN):
        pl.when((place == 1) & (ctx >= s))(g_copies[s - 1].start)

    back = one_hot((part, part), lambda r: (lax.rem(r, HEADS) * group
                   + lax.rem(lax.div(r, HEADS), group)) * tokens + lax.div(r, slots))
    for k in range(1, HEADS):
        pltpu.make_async_remote_copy(
            src_ref=dq_out.at[k - 1], dst_ref=dq_in.at[head_at(k)],
            send_sem=dq_send.at[k - 1], recv_sem=dq_recv.at[k - 1],
            device_id={"ctx": ctx, "head": head_at(-k)}, device_id_type=MESH,
        ).wait_recv()
    pl.when((place == 2) & (ctx >= 3))(g_copies[2].start)
    for i in range(width // tokens):
        pieces = []
        for a in range(slots):
            g, j = divmod(a, group)
            pieces.append(dq_in[g, j * width + i * tokens:j * width + (i + 1) * tokens])
        dq_ref[i * part:(i + 1) * part] = jnp.dot(
            back, jnp.concatenate(pieces, axis=0), preferred_element_type=F32
        ).astype(BF16)

    for s in range(1, SPAN):
        later(s)(g_copies[s - 1].wait_recv)
    for i in range(2):
        acc = mine[i]
        for s in range(1, SPAN):
            acc = acc + g_in[s - 1, i].astype(F32)
        dkv_ref[i] = acc.astype(BF16)
    for s in range(1, SPAN):
        pl.when(direct(s))(kv_copies[s - 1].wait_send)
        earlier(s)(g_copies[s - 1].wait_send)
    relay()(passed_on.wait_send)
    for copy in qo_copies + dq_copies:
        copy.wait_send()


def store(dq_ref, dkv_ref, dq_hbm, dk_hbm, dv_hbm, sems):
    pairs = ((dq_ref, dq_hbm), (dkv_ref.at[0], dk_hbm), (dkv_ref.at[1], dv_hbm))
    copies = [pltpu.make_async_copy(a, b, sems.at[i]) for i, (a, b) in enumerate(pairs)]
    for copy in copies:
        copy.start()
    for copy in copies:
        copy.wait()


def on_device(queries, keys, values, out_grad, lengths):
    width, group, heads, depth = queries.shape
    rows = group * width
    total_q = heads * rows
    hbm = pl.BlockSpec(memory_space=pltpu.HBM)
    vmem = pl.BlockSpec(memory_space=pltpu.VMEM)
    dma = pltpu.SemaphoreType.DMA((3,))
    dq, dkv = pl.pallas_call(
        kernel,
        out_shape=(
            pltpu.VMEM((total_q, depth), BF16),
            pltpu.VMEM((2, width, depth), BF16),
        ),
        in_specs=[hbm] * 5,
        out_specs=(vmem, vmem),
        scratch_shapes=[
            pltpu.VMEM((1, lengths.shape[0]), I32),
            pltpu.VMEM((total_q, depth), BF16),
            pltpu.VMEM((heads * width, depth), BF16),
            pltpu.VMEM((heads * width, depth), BF16),
            pltpu.VMEM((total_q, depth), BF16),
            pltpu.VMEM((heads, 2, rows, depth), BF16),
            pltpu.VMEM((2, width, depth), BF16),
            pltpu.VMEM((HEADS - 1, 2, rows, depth), BF16),
            pltpu.VMEM((SPAN - 1, 2, width, depth), BF16),
            pltpu.VMEM((depth, SPAN * width), BF16),
            pltpu.VMEM((SPAN, width, total_q), F32),
            pltpu.VMEM((SPAN, width, total_q), F32),
            pltpu.VMEM((SPAN * width, total_q), BF16),
            pltpu.VMEM((SPAN, 1, total_q), F32),
            pltpu.VMEM((SPAN, 1, total_q), F32),
            pltpu.VMEM((SPAN, 1, total_q), F32),
            pltpu.VMEM((SPAN - 1, 2, width, depth), BF16),
            pltpu.VMEM((SPAN - 1, 2, width, depth), BF16),
            pltpu.VMEM((HEADS - 1, rows, depth), BF16),
            pltpu.VMEM((HEADS, rows, depth), BF16),
            pltpu.SemaphoreType.DMA((5,)),
        ] + [dma] * 9,
        compiler_params=pltpu.CompilerParams(
            collective_id=0, has_side_effects=True, vmem_limit_bytes=62 * 2 ** 20
        ),
    )(
        lengths.reshape(1, -1),
        queries.reshape(total_q, depth),
        keys.reshape(heads * width, depth),
        values.reshape(heads * width, depth),
        out_grad.reshape(total_q, depth),
    )
    vin = pl.BlockSpec(memory_space=pltpu.VMEM)
    dq, dk, dv = pl.pallas_call(
        store,
        out_shape=(
            jax.ShapeDtypeStruct((total_q, depth), BF16),
            jax.ShapeDtypeStruct((width, depth), BF16),
            jax.ShapeDtypeStruct((width, depth), BF16),
        ),
        in_specs=[pl.BlockSpec(memory_space=pl.ANY)] * 2,
        out_specs=(hbm, hbm, hbm),
        scratch_shapes=[pltpu.SemaphoreType.DMA((3,))],
        compiler_params=pltpu.CompilerParams(vmem_limit_bytes=4 * 2 ** 20),
    )(dq, dkv)
    return dq.reshape(queries.shape), dk[:, None, :], dv[:, None, :]


def solution(mesh):
    in_specs = (
        P("ctx", "head", None, None),
        P("ctx", None, None),
        P("ctx", None, None),
        P("ctx", "head", None, None),
        P(),
    )
    out_specs = (P("ctx", "head", None, None), P("ctx", "head", None), P("ctx", "head", None))
    return jax.shard_map(
        on_device, mesh=mesh, in_specs=in_specs, out_specs=out_specs, check_vma=False
    )
```

```python
import jax
import jax.numpy as jnp
from jax import lax
from jax.experimental import pallas as pl
from jax.experimental.pallas import tpu as pltpu
from jax.sharding import PartitionSpec as P

SPAN = 4
ROW = 16
HEADS = 4
LOWEST = -1e30
LOG2E = 1.4426950408889634
MESH = pl.DeviceIdType.MESH
NT = (((1,), (1,)), ((), ()))
BF16, F32, I32 = jnp.bfloat16, jnp.float32, jnp.int32


def one_hot(shape, column_of_row):
    row = lax.broadcasted_iota(I32, shape, 0)
    column = lax.broadcasted_iota(I32, shape, 1)
    return jnp.where(column == column_of_row(row), 1.0, 0.0).astype(BF16)


def kernel(
    len_hbm, q_hbm, k_hbm, v_hbm, o_hbm,
    dq_ref, dkv_ref,
    len_in, q_in, k_in, v_in, o_in,
    qo_own, kv_own, qo_all, kv_all, kt_all, e_all, dp_all, ds_all, m_all, t_all, w_all,
    g_out, g_in, dq_out, dq_in,
    local, qo_send, qo_recv, kv_send, relay_send, kv_recv, g_send, g_recv, dq_send, dq_recv,
):
    ctx = lax.axis_index("ctx")
    head = lax.axis_index("head")
    count = lax.axis_size("ctx")
    place = lax.rem(ctx, ROW)
    width, depth = kv_own.shape[1:]
    rows = qo_own.shape[2]
    group = rows // width
    slots = group * HEADS
    factor = depth ** -0.5

    def ctx_at(shift):
        return lax.rem(ctx + (shift + count), count)

    def head_at(shift):
        return lax.rem(head + (shift + HEADS), HEADS)

    def fetch(source, target, index):
        copy = pltpu.make_async_copy(source, target, local.at[index])
        copy.start()
        return copy

    def remote(source, target, sems, index, ctx_shift=0, head_shift=0):
        sender, receiver = index if isinstance(index, tuple) else (index, index)
        return pltpu.make_async_remote_copy(
            src_ref=source, dst_ref=target, send_sem=sems[0].at[sender], recv_sem=sems[1].at[receiver],
            device_id={"ctx": ctx_at(ctx_shift), "head": head_at(head_shift)}, device_id_type=MESH,
        )

    def send(*args, **kwargs):
        copy = remote(*args, **kwargs)
        copy.start()
        return copy

    def later(s):
        return pl.when(ctx + s < count)

    def earlier(s):
        return pl.when(ctx >= s)

    def direct(s):
        return (ctx + s < count) & ((place + s != ROW) | (s != 2))

    def relay():
        return pl.when((place == 1) & (ctx > ROW))

    k_copy = fetch(k_hbm, k_in, 0)
    v_copy = fetch(v_hbm, v_in, 1)
    barrier = pltpu.get_barrier_semaphore()
    for s in range(1, SPAN):
        @earlier(s)
        def _(s=s):
            pl.semaphore_signal(
                barrier, inc=1, device_id={"ctx": ctx_at(-s), "head": head}, device_id_type=MESH
            )
    for k in range(1, HEADS):
        pl.semaphore_signal(
            barrier, inc=1, device_id={"ctx": ctx, "head": head_at(k)}, device_id_type=MESH
        )
    q_copy = fetch(q_hbm, q_in, 2)
    o_copy = fetch(o_hbm, o_in, 3)
    len_copy = fetch(len_hbm, len_in, 4)

    part = 2 * width
    tokens = part // HEADS
    pick = one_hot((tokens, part), lambda t: t * HEADS + head)
    k_copy.wait()
    v_copy.wait()
    for i in range(width // tokens):
        both = jnp.concatenate([k_in[i * part:(i + 1) * part], v_in[i * part:(i + 1) * part]], axis=1)
        both = jnp.dot(pick, both, preferred_element_type=F32).astype(BF16)
        kv_own[0, i * tokens:(i + 1) * tokens] = both[:, :depth]
        kv_own[1, i * tokens:(i + 1) * tokens] = both[:, depth:]

    for s in range(SPAN):
        @pl.when(ctx + s < count if s == SPAN - 1 else ctx + s == count - 1)
        def _(s=s):
            pl.semaphore_wait(barrier, HEADS - 1 + s)

    for s in range(1, SPAN):
        @pl.when(ctx < s)
        def _(s=s):
            kv_all[s - 1] = jnp.zeros((2, width, depth), BF16)

        @pl.when(ctx + s >= count)
        def _(s=s):
            g_in[s - 1] = jnp.zeros((2, width, depth), BF16)

    kv_copies = [
        remote(kv_own, kv_all.at[s - 1], (kv_send, kv_recv), s - 1, ctx_shift=s) for s in range(1, SPAN)
    ]
    g_copies = [
        remote(g_out.at[s - 1], g_in.at[s - 1], (g_send, g_recv), s - 1, ctx_shift=-s)
        for s in range(1, SPAN)
    ]
    passed_on = remote(kv_all.at[2], kv_all.at[1], (relay_send, kv_recv), (0, 1), ctx_shift=-1)
    for s in (3, 1):
        pl.when(direct(s) & (place == ROW - 2))(kv_copies[s - 1].start)
    for s in (1, 2, 3):
        pl.when(direct(s) & (place == ROW - 3))(kv_copies[s - 1].start)
    for s in (1, 2, 3):
        pl.when(direct(s) & ((place < ROW - 3) | (place == ROW - 1)))(kv_copies[s - 1].start)

    tokens = part // slots
    order = one_hot((part, part), lambda r: lax.rem(r, tokens) * slots
                    + lax.rem(lax.div(r, tokens), group) * HEADS + lax.div(r, tokens * group))
    q_copy.wait()
    o_copy.wait()
    for i in range(width // tokens):
        both = jnp.concatenate([q_in[i * part:(i + 1) * part], o_in[i * part:(i + 1) * part]], axis=1)
        both = jnp.dot(order, both, preferred_element_type=F32).astype(BF16)
        for a in range(slots):
            g, j = divmod(a, group)
            here = slice(j * width + i * tokens, j * width + (i + 1) * tokens)
            qo_own[g, 0, here] = both[a * tokens:(a + 1) * tokens, :depth]
            qo_own[g, 1, here] = both[a * tokens:(a + 1) * tokens, depth:]
    qo_copies = [
        send(qo_own.at[head_at(k)], qo_all.at[k - 1], (qo_send, qo_recv), k - 1, head_shift=k)
        for k in range(1, HEADS)
    ]

    len_copy.wait()
    down = lax.broadcasted_iota(I32, (width, width), 0)
    across = lax.broadcasted_iota(I32, (width, width), 1)
    spread = jnp.broadcast_to(len_in[...], (width, width)).astype(F32)
    ends = jnp.sum(jnp.where(across <= down, spread, 0.0), axis=1, keepdims=True)
    own = jnp.sum(jnp.where(across == down, spread, 0.0), axis=1, keepdims=True)
    query_pos = ctx * width + across
    start = jnp.sum(
        jnp.where(ends <= query_pos.astype(F32), own, 0.0), axis=0, keepdims=True
    ).astype(I32)


    def qo(k):
        return qo_own.at[head] if k == 0 else qo_all.at[k - 1]

    def kv(s):
        return kv_own if s == 0 else kv_all.at[s - 1]

    scale = factor * LOG2E
    for s in (0, 1, 3, 2):
        if s:
            earlier(s)(kv_copies[s - 1].wait_recv)
            if s == 3:
                relay()(passed_on.start)
        keys = kv(s)[0]
        values = kv(s)[1]
        kt_all[:, s * width:(s + 1) * width] = keys.T
        key_pos = (ctx - s) * width + down
        allowed = (key_pos >= start) & (key_pos <= query_pos)
        bias = jnp.where(allowed, 0.0, LOWEST)
        bias = jnp.concatenate([bias] * group, axis=1)
        for k in range(HEADS):
            if s == 0 and k:
                qo_copies[k - 1].wait_recv()
            cols = slice(k * rows, (k + 1) * rows)
            score = lax.dot_general(keys, qo(k)[0], NT, preferred_element_type=F32) + bias
            dprob = lax.dot_general(values, qo(k)[1], NT, preferred_element_type=F32)
            peak = jnp.max(score, axis=0, keepdims=True)
            expo = jnp.exp2((score - peak) * scale)
            m_all[s, :, cols] = peak
            t_all[s, :, cols] = jnp.sum(expo, axis=0, keepdims=True)
            w_all[s, :, cols] = jnp.sum(expo * dprob, axis=0, keepdims=True)
            e_all[s, :, cols] = expo
            dp_all[s, :, cols] = dprob

    peaks = [m_all[s] for s in range(SPAN)]
    peak = jnp.maximum(jnp.maximum(peaks[0], peaks[1]), jnp.maximum(peaks[2], peaks[3]))
    shares = [jnp.exp2((p - peak) * scale) for p in peaks]
    total = sum(t_all[s] * shares[s] for s in range(SPAN))
    inverse = 1.0 / total
    delta = sum(w_all[s] * shares[s] for s in range(SPAN)) * inverse
    shares = [share * inverse for share in shares]

    mine = None
    for s in (1, 2, 3, 0):
        keys_part = jnp.zeros((width, depth), F32)
        values_part = jnp.zeros((width, depth), F32)
        for k in range(HEADS):
            cols = slice(k * rows, (k + 1) * rows)
            prob = e_all[s, :, cols] * shares[s][:, cols]
            dscore = (prob * (dp_all[s, :, cols] - delta[:, cols])).astype(BF16)
            ds_all[s * width:(s + 1) * width, cols] = dscore
            keys_part += jnp.dot(dscore, qo(k)[0], preferred_element_type=F32)
            values_part += jnp.dot(prob.astype(BF16), qo(k)[1], preferred_element_type=F32)
        keys_part = keys_part * factor
        if s:
            g_out[s - 1, 0] = keys_part.astype(BF16)
            g_out[s - 1, 1] = values_part.astype(BF16)
            pl.when((ctx >= s) & ((place == 0) | (place >= s)))(g_copies[s - 1].start)
        else:
            mine = (keys_part, values_part)

    dq_copies = []
    for k in (2, 1, 3, 0):
        cols = slice(k * rows, (k + 1) * rows)
        dq = jnp.dot(kt_all[...], ds_all[:, cols], preferred_element_type=F32)
        dq = (dq.T * factor).astype(BF16)
        if k:
            dq_out[k - 1] = dq
            dq_copies.append(
                send(dq_out.at[k - 1], dq_in.at[head], (dq_send, dq_recv), k - 1, head_shift=-k)
            )
        else:
            dq_in[head] = dq


    pl.when((place == 1) & (ctx >= 2))(g_copies[1].start)

    back = one_hot((part, part), lambda r: (lax.rem(r, HEADS) * group
                   + lax.rem(lax.div(r, HEADS), group)) * tokens + lax.div(r, slots))
    for k in range(1, HEADS):
        pltpu.make_async_remote_copy(
            src_ref=dq_out.at[k - 1], dst_ref=dq_in.at[head_at(k)],
            send_sem=dq_send.at[k - 1], recv_sem=dq_recv.at[k - 1],
            device_id={"ctx": ctx, "head": head_at(-k)}, device_id_type=MESH,
        ).wait_recv()
    pl.when(((place == 1) | (place == 2)) & (ctx >= 3))(g_copies[2].start)
    for i in range(width // tokens):
        pieces = []
        for a in range(slots):
            g, j = divmod(a, group)
            pieces.append(dq_in[g, j * width + i * tokens:j * width + (i + 1) * tokens])
        dq_ref[i * part:(i + 1) * part] = jnp.dot(
            back, jnp.concatenate(pieces, axis=0), preferred_element_type=F32
        ).astype(BF16)

    for s in range(1, SPAN):
        later(s)(g_copies[s - 1].wait_recv)
    for i in range(2):
        acc = mine[i]
        for s in range(1, SPAN):
            acc = acc + g_in[s - 1, i].astype(F32)
        dkv_ref[i] = acc.astype(BF16)
    for s in range(1, SPAN):
        pl.when(direct(s))(kv_copies[s - 1].wait_send)
        earlier(s)(g_copies[s - 1].wait_send)
    relay()(passed_on.wait_send)
    for copy in qo_copies + dq_copies:
        copy.wait_send()


def store(dq_ref, dkv_ref, dq_hbm, dk_hbm, dv_hbm, sems):
    pairs = ((dq_ref, dq_hbm), (dkv_ref.at[0], dk_hbm), (dkv_ref.at[1], dv_hbm))
    copies = [pltpu.make_async_copy(a, b, sems.at[i]) for i, (a, b) in enumerate(pairs)]
    for copy in copies:
        copy.start()
    for copy in copies:
        copy.wait()


def on_device(queries, keys, values, out_grad, lengths):
    width, group, heads, depth = queries.shape
    rows = group * width
    total_q = heads * rows
    hbm = pl.BlockSpec(memory_space=pltpu.HBM)
    vmem = pl.BlockSpec(memory_space=pltpu.VMEM)
    dma = pltpu.SemaphoreType.DMA((3,))
    dq, dkv = pl.pallas_call(
        kernel,
        out_shape=(
            pltpu.VMEM((total_q, depth), BF16),
            pltpu.VMEM((2, width, depth), BF16),
        ),
        in_specs=[hbm] * 5,
        out_specs=(vmem, vmem),
        scratch_shapes=[
            pltpu.VMEM((1, lengths.shape[0]), I32),
            pltpu.VMEM((total_q, depth), BF16),
            pltpu.VMEM((heads * width, depth), BF16),
            pltpu.VMEM((heads * width, depth), BF16),
            pltpu.VMEM((total_q, depth), BF16),
            pltpu.VMEM((heads, 2, rows, depth), BF16),
            pltpu.VMEM((2, width, depth), BF16),
            pltpu.VMEM((HEADS - 1, 2, rows, depth), BF16),
            pltpu.VMEM((SPAN - 1, 2, width, depth), BF16),
            pltpu.VMEM((depth, SPAN * width), BF16),
            pltpu.VMEM((SPAN, width, total_q), F32),
            pltpu.VMEM((SPAN, width, total_q), F32),
            pltpu.VMEM((SPAN * width, total_q), BF16),
            pltpu.VMEM((SPAN, 1, total_q), F32),
            pltpu.VMEM((SPAN, 1, total_q), F32),
            pltpu.VMEM((SPAN, 1, total_q), F32),
            pltpu.VMEM((SPAN - 1, 2, width, depth), BF16),
            pltpu.VMEM((SPAN - 1, 2, width, depth), BF16),
            pltpu.VMEM((HEADS - 1, rows, depth), BF16),
            pltpu.VMEM((HEADS, rows, depth), BF16),
            pltpu.SemaphoreType.DMA((5,)),
        ] + [dma] * 9,
        compiler_params=pltpu.CompilerParams(
            collective_id=0, has_side_effects=True, vmem_limit_bytes=62 * 2 ** 20
        ),
    )(
        lengths.reshape(1, -1),
        queries.reshape(total_q, depth),
        keys.reshape(heads * width, depth),
        values.reshape(heads * width, depth),
        out_grad.reshape(total_q, depth),
    )
    vin = pl.BlockSpec(memory_space=pltpu.VMEM)
    dq, dk, dv = pl.pallas_call(
        store,
        out_shape=(
            jax.ShapeDtypeStruct((total_q, depth), BF16),
            jax.ShapeDtypeStruct((width, depth), BF16),
            jax.ShapeDtypeStruct((width, depth), BF16),
        ),
        in_specs=[pl.BlockSpec(memory_space=pl.ANY)] * 2,
        out_specs=(hbm, hbm, hbm),
        scratch_shapes=[pltpu.SemaphoreType.DMA((3,))],
        compiler_params=pltpu.CompilerParams(vmem_limit_bytes=4 * 2 ** 20),
    )(dq, dkv)
    return dq.reshape(queries.shape), dk[:, None, :], dv[:, None, :]


def solution(mesh):
    in_specs = (
        P("ctx", "head", None, None),
        P("ctx", None, None),
        P("ctx", None, None),
        P("ctx", "head", None, None),
        P(),
    )
    out_specs = (P("ctx", "head", None, None), P("ctx", "head", None), P("ctx", "head", None))
    return jax.shard_map(
        on_device, mesh=mesh, in_specs=in_specs, out_specs=out_specs, check_vma=False
    )
```
